128 devices in a mesh: replica: 16 (over x, z_lo, core), tensor: 8 (over z_hi, y).
Axes of the slice: x: 4, y: 4, z: 4 (z_hi: 2, z_lo: 2; z = z_hi * 2 + z_lo), core: 2. Of those that a mesh axis runs over, the one named last changes fastest.
Arguments:
- hidden: bfloat16 [4, 128, 8192], P(None, 'replica'), may hold values from -6 to 6
- query_weight: bfloat16 [8192, 4096], P(None, 'tensor'), may hold values from -0.0625 to 0.0625
- keyval_weight: bfloat16 [2, 8192, 1024], P(None, None, 'tensor'), may hold values from -0.0625 to 0.0625
- output_weight: bfloat16 [4096, 8192], P('tensor'), may hold values from -0.09375 to 0.09375
- adapter_down_stack: bfloat16 [3, 8192, 64], P(None, 'replica'), may hold values from -0.0625 to 0.0625
- adapter_query_up: bfloat16 [64, 4096], P(None, 'replica'), may hold values from -0.75 to 0.75
- adapter_keyval_up: bfloat16 [2, 64, 1024], P(None, None, 'replica'), may hold values from -0.75 to 0.75
- adapter_output_down: bfloat16 [4096, 64], P('replica'), may hold values from -0.09375 to 0.09375
- adapter_output_up: bfloat16 [64, 8192], P(None, 'replica'), may hold values from -0.75 to 0.75
- owner: int32 [16], replicated, may hold values from 0 to 15, each once
- key_cache_rows: bfloat16 [128, 1024, 1024], P('replica', None, 'tensor'), may hold values from -150 to 150
- value_cache_rows: bfloat16 [128, 1024, 1024], P('replica', None, 'tensor'), may hold values from -6 to 6
- lengths: int32 [128], P('replica'), may hold values from 1 to 1024, 81920 in all
Outputs:
- block_out: bfloat16 [4, 128, 8192], P(None, 'replica', 'tensor')
The draws below stay inside these ranges and needn't reach their ends.
All inputs are finite; a program needn't handle non-finite values. No bound on the sum of `lengths` on one device may be relied on, other than what follows from the above.
Results may differ from the reference program's by a relative error of at most 0.018.
Values may be sent and summed in bfloat16 or wider, within the bound.
A program may use at most 128 MiB of HBM per device.

```python
import math
import jax
import jax.numpy as jnp
import numpy as np
from jax import lax

MODEL_WIDTH = 8192
KV_HEADS = 8
HEAD_DIM = 128
ADAPTER_RANK = 64
STEPS = 4
LEN = 1024
ROWS = 128
QUERY_FEATURES = 4096
KEY_FEATURES = 1024
N_REPLICA = 16


def draw_key_cache_rows(key, part):
    key = jax.random.fold_in(key, 11)
    base_key = jax.random.fold_in(key, 0)
    values = jax.random.truncated_normal(base_key, -5.0, 5.0, (ROWS, LEN, KV_HEADS * HEAD_DIM), jnp.float32)
    return values.astype(jnp.bfloat16)


def block_scale(key, shape, cuts, low, largest):
    level = 1.0
    for dim, parts in cuts:
        steps = jax.random.uniform(jax.random.fold_in(jax.random.fold_in(key, 6), dim), (parts,), jnp.float32, low / len(cuts), largest / len(cuts))
        level = level * jnp.repeat(jnp.exp(steps), shape[dim] // parts).reshape((-1,) + (1,) * (len(shape) - 1 - dim))
    return level


def split_up(count, total, reach, skew):
    loads = [(1 << 20) // math.isqrt(rank ** skew) + 1 for rank in range(2, count + 1)]
    rest, holding = total - reach - (count - 1), [1] * (count - 1)
    while rest > 0:
        free = [i for i in range(count - 1) if holding[i] < reach]
        whole, budget = sum([loads[i] for i in free]), rest
        for i in free:
            extra = min(reach - holding[i], max(1, budget * loads[i] // whole), rest)
            holding[i] = holding[i] + extra
            rest = rest - extra
    return np.array([reach] + holding)


def ragged_sizes(rng, count, total, most, skew):
    if count == 2:
        one = jax.random.randint(rng, (), max(1, total - most), min(most, total - 1) + 1)
        return jnp.stack([one, total - one])
    tallies = jnp.asarray(split_up(count, total, most, skew), jnp.int32)
    twos = (count - 1) // 2
    source_of, taker = tallies[1:1 + 2 * twos:2], tallies[2:2 + 2 * twos:2]
    margin = jnp.minimum(source_of - 1, most - taker)
    passed = jax.random.randint(jax.random.fold_in(rng, 1), (twos,), 0, 1 << 20) % (margin + 1)
    tallies = tallies.at[1:1 + 2 * twos:2].set(source_of - passed).at[2:2 + 2 * twos:2].set(taker + passed)
    return tallies[jax.random.permutation(jax.random.fold_in(rng, 2), count)]


def gaussian(stream_key, shape, spread, reach, cuts=(), kind=jnp.bfloat16):
    level = block_scale(stream_key, shape, cuts, -0.22, 0.18) if cuts else 1.0
    entries = jax.random.normal(stream_key, shape, jnp.float32) * spread * level
    return jnp.minimum(jnp.maximum(entries, -reach), reach).astype(kind)


def setup_inputs(seed: int = 0) -> dict:
    splits = jax.random.split(jax.random.key(seed), 14)
    hidden = gaussian(splits[0], (STEPS, ROWS, MODEL_WIDTH), 1.0, 6.0, ((1, 16),))
    query_weight = gaussian(splits[1], (MODEL_WIDTH, QUERY_FEATURES), MODEL_WIDTH ** -0.5, 0.0625, ((1, 8),))
    keyval_weight = gaussian(splits[2], (2, MODEL_WIDTH, KEY_FEATURES), MODEL_WIDTH ** -0.5, 0.0625, ((2, 8),))
    output_weight = gaussian(splits[3], (QUERY_FEATURES, MODEL_WIDTH), QUERY_FEATURES ** -0.5, 0.09375, ((0, 8),))
    adapter_down_stack = gaussian(splits[4], (3, MODEL_WIDTH, ADAPTER_RANK), MODEL_WIDTH ** -0.5, 0.0625, ((1, 16),))
    adapter_query_up = gaussian(splits[5], (ADAPTER_RANK, QUERY_FEATURES), ADAPTER_RANK ** -0.5, 0.75, ((1, 16),))
    adapter_keyval_up = gaussian(splits[6], (2, ADAPTER_RANK, KEY_FEATURES), ADAPTER_RANK ** -0.5, 0.75, ((2, 16),))
    adapter_output_down = gaussian(splits[7], (QUERY_FEATURES, ADAPTER_RANK), QUERY_FEATURES ** -0.5, 0.09375, ((0, 16),))
    adapter_output_up = gaussian(splits[8], (ADAPTER_RANK, MODEL_WIDTH), ADAPTER_RANK ** -0.5, 0.75, ((1, 16),))
    owner = jax.random.permutation(splits[9], N_REPLICA).astype(jnp.int32)
    key_cache_rows = draw_key_cache_rows(jax.random.fold_in(splits[13], 71), 0)
    value_cache_rows = gaussian(splits[11], (ROWS, LEN, KEY_FEATURES), 1.0, 6.0, ((0, 16), (2, 8)))
    lengths = ragged_sizes(splits[12], ROWS, ROWS * LEN * 5 // 8, LEN, 2).astype(jnp.int32)
    return dict(hidden=hidden, query_weight=query_weight, keyval_weight=keyval_weight, output_weight=output_weight, adapter_down_stack=adapter_down_stack, adapter_query_up=adapter_query_up, adapter_keyval_up=adapter_keyval_up, adapter_output_down=adapter_output_down, adapter_output_up=adapter_output_up, owner=owner, key_cache_rows=key_cache_rows, value_cache_rows=value_cache_rows, lengths=lengths)


adapter_scale = 0.5
masked_score = -1e+30

def recover_weight(stored, owner, reduce_axis):
    count = owner.shape[0]
    block_size = stored.shape[reduce_axis] // count
    block_shape = stored.shape[:reduce_axis] + (count, block_size) + stored.shape[reduce_axis + 1:]
    blocks = jnp.take(stored.reshape(block_shape), owner, axis=reduce_axis)
    return blocks.reshape(stored.shape)

def combine_block(frozen_weight, down_factor, up_factor):
    rank_update = jnp.dot(down_factor, up_factor, preferred_element_type=jnp.float32)
    return (frozen_weight.astype(jnp.float32) + adapter_scale * rank_update).astype(jnp.bfloat16)

def reference(hidden, query_weight, keyval_weight, output_weight, adapter_down_stack, adapter_query_up, adapter_keyval_up, adapter_output_down, adapter_output_up, owner, key_cache_rows, value_cache_rows, lengths):
    stacked_down_factors = recover_weight(adapter_down_stack, owner, 1)
    query_up_factor = recover_weight(adapter_query_up, owner, 1)
    keyval_up_factor = recover_weight(adapter_keyval_up, owner, 2)
    output_down_factor = recover_weight(adapter_output_down, owner, 0)
    output_up_factor = recover_weight(adapter_output_up, owner, 1)
    merged_query = combine_block(query_weight, stacked_down_factors[0], query_up_factor)
    merged_keyval = jnp.stack([combine_block(keyval_weight[0], stacked_down_factors[1], keyval_up_factor[0]), combine_block(keyval_weight[1], stacked_down_factors[2], keyval_up_factor[1])])
    merged_out = combine_block(output_weight, output_down_factor, output_up_factor)
    steps, batch, width = hidden.shape
    inputs = hidden.reshape(steps * batch, width)
    kv_heads = key_cache_rows.shape[2] // HEAD_DIM
    group = merged_query.shape[1] // (kv_heads * HEAD_DIM)
    queries = jnp.dot(inputs, merged_query, preferred_element_type=jnp.float32).astype(jnp.bfloat16)
    queries = queries.reshape(steps, batch, kv_heads, group, HEAD_DIM).astype(jnp.float32)
    fresh = jnp.einsum('nd,cde->cne', inputs.astype(jnp.float32), merged_keyval.astype(jnp.float32)).astype(jnp.bfloat16)
    fresh = fresh.reshape(2, steps, batch, kv_heads, HEAD_DIM).astype(jnp.float32)
    new_keys = fresh[0]
    new_values = fresh[1]
    inv_scale = 1.0 / math.sqrt(HEAD_DIM)
    past_keys = key_cache_rows.reshape(batch, -1, kv_heads, HEAD_DIM).astype(jnp.float32)
    past_values = value_cache_rows.reshape(batch, -1, kv_heads, HEAD_DIM).astype(jnp.float32)
    slots = past_keys.shape[1]
    past_scores = jnp.einsum('srkgd,rlkd->srkgl', queries, past_keys) * inv_scale
    visible = jnp.arange(slots, dtype=jnp.int32)[None, :] < lengths[:, None]
    past_scores = jnp.where(visible[None, :, None, None, :], past_scores, masked_score)
    new_scores = jnp.einsum('srkgd,trkd->srkgt', queries, new_keys) * inv_scale
    causal = jnp.arange(steps, dtype=jnp.int32)[None, :] <= jnp.arange(steps, dtype=jnp.int32)[:, None]
    new_scores = jnp.where(causal[:, None, None, None, :], new_scores, masked_score)
    highest = jnp.maximum(lax.optimization_barrier(jnp.max(past_scores, -1, keepdims=True)), lax.optimization_barrier(jnp.max(new_scores, -1, keepdims=True)))
    past_exp = jnp.exp(past_scores - highest)
    new_exp = jnp.exp(new_scores - highest)
    denominator = lax.optimization_barrier(jnp.sum(past_exp, -1, keepdims=True)) + lax.optimization_barrier(jnp.sum(new_exp, -1, keepdims=True))
    past_weights = (past_exp / denominator).astype(jnp.bfloat16).astype(jnp.float32)
    new_weights = (new_exp / denominator).astype(jnp.bfloat16).astype(jnp.float32)
    context = jnp.einsum('srkgl,rlkd->srkgd', past_weights, past_values) + jnp.einsum('srkgt,trkd->srkgd', new_weights, new_values)
    context = context.astype(jnp.bfloat16).reshape(steps * batch, -1)
    result = jnp.dot(context, merged_out, preferred_element_type=jnp.float32)
    return result.reshape(steps, batch, width).astype(jnp.bfloat16)
```

```python
import math

import jax
import jax.numpy as jnp
from jax import lax
from jax.experimental import pallas as pl
from jax.experimental.pallas import tpu as pltpu
from jax.sharding import PartitionSpec as P

MESH = pl.DeviceIdType.MESH
BF16 = jnp.bfloat16
F32 = jnp.float32
HEAD_DIM = 128
SCALE = 0.5
MASKED = -1e30
R, T = 16, 8
K_PARTS = 4


def kernel(
    owner, lengths, hid, wq, wkv, wo, dstk, qup, kvup, odn, oup, kc, vc,
    out_ref,
    hid_v, wq_v, wkv_v, wo_v, k_v, v_v, d_v, qup_v, kvup_v, odn_v, oup_v, upk, odp,
    p1s, p1r, p1os, p1or, hc, hcs, dc, p2s, p2r, p2os, p2or,
    uqk, uv, q_s, kn_s, vn_s, acc_q, acc_kv, ctx_s, cx, do_v, uo_v, rss, rsr,
    small_sem, q_sem, kv_sem, cache_sem, wo_sem, hc_sem,
    p1_ss, p1_rs, p1o_ss, p1o_rs, p2_ss, p2_rs, p2o_ss, p2o_rs, rs_ss, rs_rs,
):
    r, t = lax.axis_index("replica"), lax.axis_index("tensor")
    x, zl, c = r // 4, lax.rem(r // 2, 2), lax.rem(r, 2)
    other = r + 1 - 2 * c
    mine = t * 2 + c
    rows = 8192 // K_PARTS

    t64 = pl.multiple_of(t * 64, 64)
    small = [
        pltpu.make_async_copy(dstk.at[:, pl.ds(t64, 64), :], d_v, small_sem.at[0]),
        pltpu.make_async_copy(qup, qup_v, small_sem.at[1]),
        pltpu.make_async_copy(kvup, kvup_v, small_sem.at[2]),
        pltpu.make_async_copy(odn, odn_v, small_sem.at[3]),
        pltpu.make_async_copy(oup, oup_v, small_sem.at[4]),
    ]
    hid_copy = pltpu.make_async_copy(hid, hid_v, small_sem.at[5])
    for copy in small:
        copy.start()
    hid_copy.start()

    def q_copies(i):
        at = pl.ds(pl.multiple_of(i * rows, rows), rows)
        return [
            pltpu.make_async_copy(wq.at[at, :], wq_v.at[at, :], q_sem.at[i]),
            pltpu.make_async_copy(wkv.at[0, at, :], wkv_v.at[at, pl.ds(0, 128)], kv_sem.at[0, i]),
            pltpu.make_async_copy(wkv.at[1, at, :], wkv_v.at[at, pl.ds(128, 128)], kv_sem.at[1, i]),
        ]

    for i in range(K_PARTS):
        for copy in q_copies(i):
            copy.start()
    cache = [
        pltpu.make_async_copy(kc, k_v.at[:, pl.ds(0, 1024), :], cache_sem.at[0]),
        pltpu.make_async_copy(vc, v_v.at[:, pl.ds(0, 1024), :], cache_sem.at[1]),
    ]
    for copy in cache:
        copy.start()
    heads = [lax.rem(t + i, T) for i in (6, 2, 5, 3, 4, 7, 1, 0)]
    wo_copies = [
        pltpu.make_async_copy(
            wo.at[:, pl.ds(pl.multiple_of(heads[i] * 1024, 1024), 1024)], wo_v.at[i], wo_sem.at[i]
        )
        for i in range(T)
    ]
    for copy in wo_copies:
        copy.start()

    barrier = pltpu.get_barrier_semaphore()
    ring = [
        (lax.rem(x + dx, 4) * 4 + (zl if dz == 0 else 1 - zl) * 2 + (c if dc_ == 0 else 1 - c), t)
        for dx, dz in ((2, 1), (2, 0), (1, 1), (3, 1), (1, 0), (3, 0), (0, 1), (0, 0))
        for dc_ in (0, 1)
        if dx or dz or dc_
    ]
    cross = [
        (r if dc_ == 0 else other, lax.rem(t + i, T))
        for i in (6, 2, 5, 3, 4, 7, 1, 0)
        for dc_ in (0, 1)
        if i or dc_
    ]
    greeted = ring + [(rr, tt) for j, (rr, tt) in enumerate(cross) if j < 14]
    for peer in greeted:
        pl.semaphore_signal(barrier, inc=1, device_id=peer, device_id_type=MESH)

    for copy in small:
        copy.wait()
    lane = lax.broadcasted_iota(jnp.int32, (16, 128), 1)
    upk[0] = qup_v[:, 0:128]
    upk[1] = qup_v[:, 128:256]
    upk[2] = jnp.concatenate([kvup_v[0], kvup_v[1]], axis=1)
    upk[3] = jnp.zeros((64, 128), BF16)
    odp[...] = jnp.concatenate([odn_v[0:128, :], odn_v[128:256, :]], axis=1)
    t32 = pl.multiple_of(lax.rem(t, 2) * 32, 32)
    u_rows = upk[t // 2, pl.ds(t32, 32), :]
    uo_rows = oup_v[pl.ds(t32, 32), pl.ds(pl.multiple_of((t // 2) * 128, 128), 128)]
    do_rows = odp[pl.ds(pl.multiple_of(lax.rem(t, 4) * 32, 32), 32), :]
    for j in range(2):
        p1s[j, 0:32, :] = jnp.concatenate(
            [d_v[0, j * 32 : j * 32 + 32, :], d_v[1, j * 32 : j * 32 + 32, :]], axis=1
        )
        p1s[j, 32:48, :] = jnp.concatenate(
            [d_v[2, j * 32 : j * 32 + 16, :], d_v[2, j * 32 + 16 : j * 32 + 32, :]], axis=1
        )
        p1s[j, 48:64, :] = u_rows[j * 16 : j * 16 + 16]
        p1os[j, 0:16, :] = uo_rows[j * 16 : j * 16 + 16]
        p1os[j, 16:32, :] = do_rows[j * 16 : j * 16 + 16]

    pl.semaphore_wait(barrier, len(greeted))

    sends = []

    def send(src, dst, ss, rs, peer):
        copy = pltpu.make_async_remote_copy(
            src_ref=src, dst_ref=dst, send_sem=ss, recv_sem=rs, device_id=peer, device_id_type=MESH
        )
        copy.start()
        sends.append(copy)

    for j, peer in enumerate(ring):
        send(p1s.at[lax.rem(peer[0], 2)], p1r.at[r], p1_ss.at[j], p1_rs.at[r], peer)
    for j, peer in enumerate(ring):
        send(p1os.at[lax.rem(peer[0], 2)], p1or.at[r], p1o_ss.at[j], p1o_rs.at[r], peer)
    p1r[r] = p1s[c]
    p1or[r] = p1os[c]

    hid_copy.wait()
    row = lax.broadcasted_iota(jnp.int32, (512, 256), 0)
    col = lax.broadcasted_iota(jnp.int32, (512, 256), 1)
    at_row = (
        lax.rem(col // 16, 4) * 128
        + lax.rem(t, 2) * 64
        + (col // 128) * 32
        + lax.rem(col // 64, 2) * 16
        + lax.rem(col, 16)
    )
    select = jnp.where(row == at_row, 1.0, 0.0).astype(BF16)
    half = pl.multiple_of((t // 2) * 128, 128)
    for g in range(4):
        wide = jnp.concatenate(
            [hid_v[:, pl.ds(pl.multiple_of((4 * g + j) * 512 + half, 128), 128)] for j in range(4)],
            axis=1,
        )
        got = jnp.dot(wide, select, preferred_element_type=F32).astype(BF16)
        low, high = got[:, 0:128], got[:, 128:256]
        hc[0, :, g * 128 : (g + 1) * 128] = jnp.where(c == 0, low, high)
        hcs[:, g * 128 : (g + 1) * 128] = jnp.where(c == 0, high, low)
    send(hcs, hc.at[1], hc_sem.at[0], hc_sem.at[1], (other, t))
    hc_copy = sends[-1]

    acc_q[...] = jnp.zeros_like(acc_q)
    acc_kv[...] = jnp.zeros_like(acc_kv)

    @pl.loop(0, K_PARTS)
    def _(i):
        for copy in q_copies(i):
            copy.wait()
        at = pl.ds(pl.multiple_of(i * rows, rows), rows)
        part = hid_v[:, at]
        acc_q[...] += jnp.dot(part, wq_v[at, :], preferred_element_type=F32)
        acc_kv[...] += jnp.dot(part, wkv_v[at, :], preferred_element_type=F32)

    for peer in ring:
        pltpu.make_async_copy(p1r.at[peer[0]], p1r.at[peer[0]], p1_rs.at[peer[0]]).wait()
    zero = jnp.zeros((16, 128), BF16)
    for s in range(R):
        of = owner[s]
        dv = p1r[of, 32:48, :]
        for h in range(2):
            at = (((s // 4) * 2 + h) * 4 + s % 4) * 16
            dc[at : at + 16, 0:128] = p1r[of, h * 16 : h * 16 + 16, :]
            keep = lane < 64 if h == 0 else lane >= 64
            dc[at : at + 16, 128:256] = jnp.where(keep, dv, zero)
    hc_copy.wait_recv()
    both = hc[...].reshape(64, 512)
    part_a = jnp.dot(both, dc[...], preferred_element_type=F32)
    packed = []
    for j in range(2):
        a = part_a[j * 32 : j * 32 + 32]
        v = a[:, 128:256]
        v = v + pltpu.roll(v, 64, 1)
        packed.append((a[:, 0:128].astype(BF16), jnp.where(lane < 64, v[0:16], v[16:32]).astype(BF16)))
    j = 0
    for i in (6, 2, 5, 3, 4, 7, 1, 0):
        to = lax.rem(t + i, T)
        first, second = p1r[owner[2 * to], 48:64, :], p1r[owner[2 * to + 1], 48:64, :]
        for dc_ in (0, 1):
            p2s[j, 0:32, :] = packed[dc_][0]
            p2s[j, 32:48, :] = packed[dc_][1]
            p2s[j, 48:64, :] = first
            p2s[j, 64:80, :] = second
            if i or dc_:
                peer = (r if dc_ == 0 else other, to)
                send(p2s.at[j], p2r.at[mine], p2_ss.at[j], p2_rs.at[mine], peer)
            else:
                p2r[mine] = p2s[j]
            j += 1

    for peer in ring:
        pltpu.make_async_copy(p1or.at[peer[0]], p1or.at[peer[0]], p1o_rs.at[peer[0]]).wait()
    j = 0
    for i in (6, 2, 5, 3, 4, 7, 1, 0):
        to = lax.rem(t + i, T)
        p2os[j, 0:32, :] = p1or[owner[2 * to]]
        p2os[j, 32:64, :] = p1or[owner[2 * to + 1]]
        for dc_ in (0, 1):
            if i or dc_:
                peer = (r if dc_ == 0 else other, to)
                send(p2os.at[j], p2or.at[mine], p2o_ss.at[2 * j + dc_], p2o_rs.at[mine], peer)
            else:
                p2or[mine] = p2os[j]
        j += 1

    k_v[:, 1040:1152, :] = jnp.zeros((8, 112, 128), BF16)
    v_v[:, 1040:1152, :] = jnp.zeros((8, 112, 128), BF16)
    kn_s[32:128, :] = jnp.zeros((96, 128), F32)
    vn_s[32:128, :] = jnp.zeros((96, 128), F32)
    uqk[0:64, 512:640] = jnp.zeros((64, 128), BF16)
    uqk[64:128, 0:512] = jnp.zeros((64, 512), BF16)

    for i in range(T):
        for dc_ in (0, 1):
            if i or dc_:
                m = lax.rem(t + i, T) * 2 + (c if dc_ == 0 else 1 - c)
                pltpu.make_async_copy(p2r.at[m], p2r.at[m], p2_rs.at[m]).wait()
    a_qk = jnp.zeros((32, 128), F32)
    a_v = jnp.zeros((16, 128), F32)
    for m in range(16):
        a_qk = a_qk + p2r[m, 0:32, :].astype(F32)
        a_v = a_v + p2r[m, 32:48, :].astype(F32)
    for m in range(12):
        g, block = m % 4, m // 4
        first, second = p2r[m, 48:64, :], p2r[m, 64:80, :]
        if block < 2:
            uqk[g * 16 : g * 16 + 16, block * 128 : block * 128 + 128] = first
            uqk[g * 16 : g * 16 + 16, 256 + block * 128 : 384 + block * 128] = second
        else:
            first, second = first.astype(F32), second.astype(F32)
            uk = jnp.where(lane < 64, first, pltpu.roll(second, 64, 1)).astype(BF16)
            uvt = jnp.where(lane < 64, pltpu.roll(first, 64, 1), second).astype(BF16)
            uqk[64 + g * 16 : 80 + g * 16, 512:640] = uk
            uv[g * 16 : g * 16 + 16, :] = uvt
            uv[64 + g * 16 : 80 + g * 16, :] = uvt
    a_v2 = jnp.concatenate([jnp.where(lane < 64, a_v, 0.0), jnp.where(lane >= 64, a_v, 0.0)], axis=0)
    d_qk = jnp.dot(a_qk.astype(BF16), uqk[...], preferred_element_type=F32)
    d_val = jnp.dot(a_v2.astype(BF16), uv[...], preferred_element_type=F32)
    q = (acc_q[...] + SCALE * d_qk[:, 0:512]).astype(BF16).astype(F32)
    for s in range(4):
        for h in range(4):
            q_s[(s * 4 + h) * 8 : (s * 4 + h) * 8 + 8, :] = q[s * 8 : s * 8 + 8, h * 128 : h * 128 + 128]
    kn_s[0:32, :] = acc_kv[:, 0:128] + SCALE * d_qk[:, 512:640]
    vn_s[0:32, :] = acc_kv[:, 128:256] + SCALE * d_val

    for copy in cache:
        copy.wait()
    where = lax.broadcasted_iota(jnp.int32, (16, 1152), 1)
    step = lax.broadcasted_iota(jnp.int32, (16, 1152), 0) // 4
    fresh = jnp.logical_and(where >= 1024, where - 1024 <= step)
    factor = math.log2(math.e) / math.sqrt(HEAD_DIM)
    for b in range(8):
        k_v[b, 1024:1040, :] = kn_s[pl.ds(b, 16, stride=8), :].astype(BF16)
        v_v[b, 1024:1040, :] = vn_s[pl.ds(b, 16, stride=8), :].astype(BF16)
    for b in range(8):
        qb = q_s[pl.ds(b, 16, stride=8), :].astype(BF16)
        scores = lax.dot_general(qb, k_v[b], (((1,), (1,)), ((), ())), preferred_element_type=F32)
        seen = jnp.logical_or(where < lengths[b], fresh)
        scores = jnp.where(seen, scores, MASKED)
        top = jnp.max(scores, axis=-1, keepdims=True)
        weights = jnp.exp2((scores - top) * factor)
        total = jnp.sum(weights, axis=-1, keepdims=True)
        got = jnp.dot(weights.astype(BF16), v_v[b], preferred_element_type=F32)
        ctx_s[pl.ds(b, 16, stride=8), :] = got / total
    for s in range(4):
        for h in range(4):
            cx[s * 8 : s * 8 + 8, h * 128 : h * 128 + 128] = ctx_s[(s * 4 + h) * 8 : (s * 4 + h) * 8 + 8, :]
    context = cx[...].astype(BF16)

    for i in range(T):
        for dc_ in (0, 1):
            if i or dc_:
                m = lax.rem(t + i, T) * 2 + (c if dc_ == 0 else 1 - c)
                pltpu.make_async_copy(p2or.at[m], p2or.at[m], p2o_rs.at[m]).wait()
    for m in range(16):
        g, block = m % 4, m // 4
        for j in range(2):
            tile = p2or[m, j * 32 : j * 32 + 16, :]
            at = j * 512 + block * 128
            uo_v[g * 16 : g * 16 + 16, at : at + 128] = tile
            uo_v[64 + g * 16 : 80 + g * 16, at : at + 128] = tile
            if m < 8:
                do_v[j, m * 16 : m * 16 + 16, :] = p2or[m, j * 32 + 16 : j * 32 + 32, :]
    lane32 = lax.broadcasted_iota(jnp.int32, (32, 128), 1)
    z_low = jnp.dot(context[:, 0:128], do_v[0], preferred_element_type=F32)
    z_low += jnp.dot(context[:, 256:384], do_v[1], preferred_element_type=F32)
    z_high = jnp.dot(context[:, 128:256], do_v[0], preferred_element_type=F32)
    z_high += jnp.dot(context[:, 384:512], do_v[1], preferred_element_type=F32)
    z = jnp.where(lane32 < 64, z_low, z_high)
    z_sent = z.astype(BF16)

    own = None
    for i in range(T):
        wo_copies[i].wait()
        part = jnp.dot(context, wo_v[i], preferred_element_type=F32)
        if i < T - 1:
            rss[i, :, 0:1024] = part.astype(BF16)
            rss[i, :, 1024:1152] = z_sent
            send(rss.at[i], rsr.at[t], rs_ss.at[i], rs_rs.at[t], (r, heads[i]))
        else:
            own = part
    for i in range(1, T):
        m = lax.rem(t + i, T)
        pltpu.make_async_copy(rsr.at[m], rsr.at[m], rs_rs.at[m]).wait()
        own = own + rsr[m, :, 0:1024].astype(F32)
        z = z + rsr[m, :, 1024:1152].astype(F32)
    own = own + SCALE * jnp.dot(z.astype(BF16), uo_v[...], preferred_element_type=F32)
    out_ref[...] = own.astype(BF16)
    for copy in sends:
        copy.wait_send()


def body(
    hidden, query_weight, keyval_weight, output_weight, adapter_down_stack, adapter_query_up,
    adapter_keyval_up, adapter_output_down, adapter_output_up, owner, key_cache_rows, value_cache_rows, lengths,
):
    steps, batch, width = hidden.shape
    rows = steps * batch
    anywhere = pl.BlockSpec(memory_space=pl.ANY)
    scalars = pl.BlockSpec(memory_space=pltpu.SMEM)
    dma = pltpu.SemaphoreType.DMA
    out = pl.pallas_call(
        kernel,
        out_shape=jax.ShapeDtypeStruct((rows, 1024), BF16),
        in_specs=[scalars, scalars] + [anywhere] * 11,
        out_specs=pl.BlockSpec(memory_space=pltpu.VMEM),
        scratch_shapes=[
            pltpu.VMEM((32, 8192), BF16),
            pltpu.VMEM((8192, 512), BF16),
            pltpu.VMEM((8192, 256), BF16),
            pltpu.VMEM((8, 512, 1024), BF16),
            pltpu.VMEM((8, 1152, 128), BF16),
            pltpu.VMEM((8, 1152, 128), BF16),
            pltpu.VMEM((3, 64, 64), BF16),
            pltpu.VMEM((64, 256), BF16),
            pltpu.VMEM((2, 64, 64), BF16),
            pltpu.VMEM((256, 64), BF16),
            pltpu.VMEM((64, 512), BF16),
            pltpu.VMEM((4, 64, 128), BF16),
            pltpu.VMEM((128, 128), BF16),
            pltpu.VMEM((2, 64, 128), BF16),
            pltpu.VMEM((16, 64, 128), BF16),
            pltpu.VMEM((2, 32, 128), BF16),
            pltpu.VMEM((16, 32, 128), BF16),
            pltpu.VMEM((2, 32, 512), BF16),
            pltpu.VMEM((32, 512), BF16),
            pltpu.VMEM((512, 256), BF16),
            pltpu.VMEM((16, 80, 128), BF16),
            pltpu.VMEM((16, 80, 128), BF16),
            pltpu.VMEM((8, 64, 128), BF16),
            pltpu.VMEM((16, 64, 128), BF16),
            pltpu.VMEM((128, 640), BF16),
            pltpu.VMEM((128, 128), BF16),
            pltpu.VMEM((128, 128), F32),
            pltpu.VMEM((128, 128), F32),
            pltpu.VMEM((128, 128), F32),
            pltpu.VMEM((32, 512), F32),
            pltpu.VMEM((32, 256), F32),
            pltpu.VMEM((128, 128), F32),
            pltpu.VMEM((32, 512), F32),
            pltpu.VMEM((2, 128, 128), BF16),
            pltpu.VMEM((128, 1024), BF16),
            pltpu.VMEM((8, 32, 1152), BF16),
            pltpu.VMEM((8, 32, 1152), BF16),
            dma((6,)), dma((K_PARTS,)), dma((2, K_PARTS)), dma((2,)), dma((T,)), dma((2,)),
            dma((15,)), dma((R,)), dma((15,)), dma((R,)), dma((16,)), dma((16,)), dma((16,)), dma((16,)),
            dma((T,)), dma((T,)),
        ],
        compiler_params=pltpu.CompilerParams(
            collective_id=0, has_side_effects=True, vmem_limit_bytes=60 * 1024 * 1024
        ),
        name="adapter_attention",
    )(
        owner, lengths, hidden.reshape(rows, width), query_weight, keyval_weight, output_weight,
        adapter_down_stack, adapter_query_up, adapter_keyval_up, adapter_output_down, adapter_output_up,
        key_cache_rows, value_cache_rows,
    )
    return out.reshape(steps, batch, 1024)


def solution(mesh):
    in_specs = (
        P(None, "replica", None),
        P(None, "tensor"),
        P(None, None, "tensor"),
        P("tensor", None),
        P(None, "replica", None),
        P(None, "replica"),
        P(None, None, "replica"),
        P("replica", None),
        P(None, "replica"),
        P(),
        P("replica", None, "tensor"),
        P("replica", None, "tensor"),
        P("replica"),
    )
    out_specs = P(None, "replica", "tensor")
    return jax.shard_map(body, mesh=mesh, in_specs=in_specs, out_specs=out_specs, check_vma=False)
```

```python
import math

import jax
import jax.numpy as jnp
from jax import lax
from jax.experimental import pallas as pl
from jax.experimental.pallas import tpu as pltpu
from jax.sharding import PartitionSpec as P

MESH = pl.DeviceIdType.MESH
BF16 = jnp.bfloat16
F32 = jnp.float32
HEAD_DIM = 128
SCALE = 0.5
MASKED = -1e30
R, T = 16, 8
K_PARTS = 4


def kernel(
    owner_any, lengths_any, hid, wq, wkv, wo, dstk, qup, kvup, odn, oup, kc, vc,
    out_ref,
    hid_v, wq_v, wkv_v, wo_v, k_v, v_v, d_v, d_t, qup_v, kvup_v, odn_v, oup_v, upk, odp,
    p1d, p1u, p1o, hc, dc, p2s, p2r, p2os, p2or,
    uqk, uv, q_s, kn_s, vn_s, acc_q, acc_kv, ctx_s, cx, do_v, uo_v, rss, rsr, zs, zr,
    owner, lengths, small_sem, q_sem, kv_sem, cache_sem, wo_sem,
    p1d_ss, p1d_rs, p1u_ss, p1u_rs, p1o_ss, p1o_rs, fwd_ss, fwd_rs, p2_ss, p2_rs, p2o_ss, p2o_rs,
    rs_ss, rs_rs, z_ss, z_rs,
):
    r, t = lax.axis_index("replica"), lax.axis_index("tensor")
    x, zl, c = r // 4, lax.rem(r // 2, 2), lax.rem(r, 2)
    zh, y = t // 4, lax.rem(t, 4)
    other = (r + 1 - 2 * c, t)
    mine = c * 8 + r // 2
    rows = 8192 // K_PARTS
    ring = [
        (lax.rem(x + dx, 4) * 4 + (zl if dz == 0 else 1 - zl) * 2 + c, t)
        for dx, dz in ((2, 1), (1, 1), (3, 1), (2, 0), (1, 0), (3, 0), (0, 1))
    ]
    slots = [c * 8 + peer[0] // 2 for peer in ring]
    heads = [
        (zh if dz == 0 else 1 - zh) * 4 + lax.rem(y + dy, 4)
        for dz, dy in ((1, 2), (1, 1), (1, 3), (0, 2), (1, 0), (0, 1), (0, 3), (0, 0))
    ]
    cross = [(r, to) for to in heads[:-1]]

    barrier = pltpu.get_barrier_semaphore()
    greeted = ring + [other] + cross
    for peer in greeted:
        pl.semaphore_signal(barrier, inc=1, device_id=peer, device_id_type=MESH)

    t128 = pl.multiple_of((t // 2) * 128, 128)
    small = [
        pltpu.make_async_copy(dstk.at[:, :, pl.ds(t128, 128)], d_v, small_sem.at[0]),
        pltpu.make_async_copy(qup, qup_v, small_sem.at[1]),
        pltpu.make_async_copy(kvup, kvup_v, small_sem.at[2]),
        pltpu.make_async_copy(odn, odn_v, small_sem.at[3]),
        pltpu.make_async_copy(oup, oup_v, small_sem.at[4]),
    ]
    hid_copy = pltpu.make_async_copy(hid, hid_v, small_sem.at[5])
    scalars = [
        pltpu.make_async_copy(owner_any, owner, small_sem.at[6]),
        pltpu.make_async_copy(lengths_any, lengths, small_sem.at[7]),
    ]
    for copy in small:
        copy.start()
    hid_copy.start()
    for copy in scalars:
        copy.start()

    def q_copies(i):
        at = pl.ds(pl.multiple_of(i * rows, rows), rows)
        return [
            pltpu.make_async_copy(wq.at[at, :], wq_v.at[at, :], q_sem.at[i]),
            pltpu.make_async_copy(wkv.at[0, at, :], wkv_v.at[at, pl.ds(0, 128)], kv_sem.at[0, i]),
            pltpu.make_async_copy(wkv.at[1, at, :], wkv_v.at[at, pl.ds(128, 128)], kv_sem.at[1, i]),
        ]

    for i in range(K_PARTS):
        for copy in q_copies(i):
            copy.start()

    k_v[:, 1040:1152, :] = jnp.zeros((8, 112, 128), BF16)
    v_v[:, 1040:1152, :] = jnp.zeros((8, 112, 128), BF16)
    kn_s[32:128, :] = jnp.zeros((96, 128), F32)
    vn_s[32:128, :] = jnp.zeros((96, 128), F32)
    uqk[0:64, 512:640] = jnp.zeros((64, 128), BF16)
    uqk[64:128, 0:512] = jnp.zeros((64, 512), BF16)

    for copy in small:
        copy.wait()
    lane = lax.broadcasted_iota(jnp.int32, (32, 128), 1)
    d_t[0] = jnp.concatenate([d_v[0], d_v[1]], axis=0).T
    d_t[1] = jnp.concatenate([d_v[2], d_v[2]], axis=0).T
    t64 = pl.multiple_of(lax.rem(t, 2) * 64, 64)
    p1d[mine, 0:64, :] = d_t[0, pl.ds(t64, 64), :]
    v_rows = d_t[1, pl.ds(t64, 64), :]
    p1d[mine, 64:96, :] = jnp.where(lane < 64, v_rows[0:32], v_rows[32:64])
    upk[0] = qup_v[:, 0:128]
    upk[1] = qup_v[:, 128:256]
    upk[2] = jnp.concatenate([kvup_v[0], kvup_v[1]], axis=1)
    upk[3] = jnp.zeros((64, 128), BF16)
    t32 = pl.multiple_of(lax.rem(t, 2) * 32, 32)
    p1u[mine] = upk[t // 2, pl.ds(t32, 32), :]
    odp[0:64, :] = odn_v[:, 0:128]
    odp[64:128, :] = odn_v[:, 128:256]
    p1o[mine, 0:32, :] = oup_v[pl.ds(t32, 32), pl.ds(t128, 128)]
    p1o[mine, 32:48, :] = odp[pl.ds(pl.multiple_of(t * 16, 16), 16), :]

    pl.semaphore_wait(barrier, len(greeted))

    sends = []

    def send(src, dst, ss, rs, peer):
        copy = pltpu.make_async_remote_copy(
            src_ref=src, dst_ref=dst, send_sem=ss, recv_sem=rs, device_id=peer, device_id_type=MESH
        )
        copy.start()
        sends.append(copy)

    def arrived(ref, sem):
        pltpu.make_async_copy(ref, ref, sem).wait()

    for j, peer in enumerate(ring):
        send(p1d.at[mine], p1d.at[mine], p1d_ss.at[j], p1d_rs.at[mine], peer)
    for j, peer in enumerate(ring):
        send(p1u.at[mine], p1u.at[mine], p1u_ss.at[j], p1u_rs.at[mine], peer)
    send(p1d.at[mine], p1d.at[mine], p1d_ss.at[7], p1d_rs.at[mine], other)

    cache = [
        pltpu.make_async_copy(kc, k_v.at[:, pl.ds(0, 1024), :], cache_sem.at[0]),
        pltpu.make_async_copy(vc, v_v.at[:, pl.ds(0, 1024), :], cache_sem.at[1]),
    ]
    for copy in cache:
        copy.start()
    wo_copies = [
        pltpu.make_async_copy(
            wo.at[:, pl.ds(pl.multiple_of(heads[i] * 1024, 1024), 1024)], wo_v.at[i], wo_sem.at[i]
        )
        for i in range(T)
    ]
    for copy in wo_copies:
        copy.start()

    hid_copy.wait()
    odd = lax.rem(t, 2) == 1
    for g in range(8):
        first = hid_v[:, pl.ds(pl.multiple_of((2 * g) * 512 + t128, 128), 128)].astype(F32)
        second = hid_v[:, pl.ds(pl.multiple_of((2 * g + 1) * 512 + t128, 128), 128)].astype(F32)
        low = jnp.where(lane < 64, first, pltpu.roll(second, 64, 1))
        high = jnp.where(lane < 64, pltpu.roll(first, 64, 1), second)
        hc[:, g * 128 : (g + 1) * 128] = jnp.where(odd, high, low).astype(BF16)

    acc_q[...] = jnp.zeros_like(acc_q)
    acc_kv[...] = jnp.zeros_like(acc_kv)

    @pl.loop(0, K_PARTS)
    def _(i):
        for copy in q_copies(i):
            copy.wait()
        at = pl.ds(pl.multiple_of(i * rows, rows), rows)
        part = hid_v[:, at]
        acc_q[...] += jnp.dot(part, wq_v[at, :], preferred_element_type=F32)
        acc_kv[...] += jnp.dot(part, wkv_v[at, :], preferred_element_type=F32)

    for j, peer in enumerate(ring):
        send(p1o.at[mine], p1o.at[mine], p1o_ss.at[j], p1o_rs.at[mine], peer)

    same = pl.ds(pl.multiple_of(c * 8, 8), 8)
    for j, slot in reversed(list(enumerate(slots))):
        arrived(p1d.at[slot], p1d_rs.at[slot])
        send(p1d.at[slot], p1d.at[slot], p1d_ss.at[8 + j], p1d_rs.at[slot], other)
    for slot in slots:
        arrived(p1u.at[slot], p1u_rs.at[slot])
    send(p1u.at[same], p1u.at[same], fwd_ss.at[0], fwd_rs.at[0], other)
    u_copy = sends[-1]

    for copy in scalars:
        copy.wait()

    for i in range(8):
        slot = (1 - c) * 8 + i
        arrived(p1d.at[slot], p1d_rs.at[slot])

    def slot_of(s):
        return lax.rem(owner[s], 2) * 8 + owner[s] // 2

    zero = jnp.zeros((32, 128), BF16)
    for s in range(R):
        of = slot_of(s)
        dc[s * 64 : s * 64 + 64, 0:128] = p1d[of, 0:64, :]
        dv = p1d[of, 64:96, :]
        dc[s * 64 : s * 64 + 32, 128:256] = jnp.where(lane < 64, dv, zero)
        dc[s * 64 + 32 : s * 64 + 64, 128:256] = jnp.where(lane < 64, zero, dv)
    part_a = jnp.dot(hc[...], dc[...], preferred_element_type=F32)
    part_v = part_a[:, 128:256]
    part_v = part_v + pltpu.roll(part_v, 64, 1)
    part_qk = part_a[:, 0:128].astype(BF16)
    part_v = jnp.where(lane[0:16] < 64, part_v[0:16], part_v[16:32]).astype(BF16)
    u_copy.wait_recv()
    for j, to in enumerate(heads):
        p2s[j, 0:32, :] = part_qk
        p2s[j, 32:48, :] = part_v
        p2s[j, 48:80, :] = p1u[slot_of(2 * to)]
        p2s[j, 80:112, :] = p1u[slot_of(2 * to + 1)]
        if j < 7:
            send(p2s.at[j], p2r.at[t], p2_ss.at[j], p2_rs.at[t], cross[j])
        else:
            p2r[t] = p2s[j]

    for slot in slots:
        arrived(p1o.at[slot], p1o_rs.at[slot])
    send(p1o.at[same], p1o.at[same], fwd_ss.at[1], fwd_rs.at[1], other)
    sends[-1].wait_recv()
    for j, to in enumerate(heads):
        p2os[j, 0:48, :] = p1o[slot_of(2 * to)]
        p2os[j, 48:96, :] = p1o[slot_of(2 * to + 1)]
        if j < 7:
            send(p2os.at[j], p2or.at[t], p2o_ss.at[j], p2o_rs.at[t], cross[j])
        else:
            p2or[t] = p2os[j]

    for m in reversed(heads[:-1]):
        arrived(p2r.at[m], p2_rs.at[m])
    a_qk = jnp.zeros((32, 128), F32)
    a_v = jnp.zeros((16, 128), F32)
    for m in range(T):
        a_qk = a_qk + p2r[m, 0:32, :].astype(F32)
        a_v = a_v + p2r[m, 32:48, :].astype(F32)
    for m in range(6):
        g, block = (m % 2) * 32, m // 2
        first, second = p2r[m, 48:80, :], p2r[m, 80:112, :]
        if block < 2:
            uqk[g : g + 32, block * 128 : block * 128 + 128] = first
            uqk[g : g + 32, 256 + block * 128 : 384 + block * 128] = second
        else:
            first, second = first.astype(F32), second.astype(F32)
            uk = jnp.where(lane < 64, first, pltpu.roll(second, 64, 1)).astype(BF16)
            uvt = jnp.where(lane < 64, pltpu.roll(first, 64, 1), second).astype(BF16)
            uqk[64 + g : 96 + g, 512:640] = uk
            uv[g : g + 32, :] = uvt
            uv[64 + g : 96 + g, :] = uvt
    low = lane[0:16] < 64
    a_v2 = jnp.concatenate([jnp.where(low, a_v, 0.0), jnp.where(low, 0.0, a_v)], axis=0)
    d_qk = jnp.dot(a_qk.astype(BF16), uqk[...], preferred_element_type=F32)
    d_val = jnp.dot(a_v2.astype(BF16), uv[...], preferred_element_type=F32)
    q = (acc_q[...] + SCALE * d_qk[:, 0:512]).astype(BF16).astype(F32)
    for s in range(4):
        for h in range(4):
            q_s[(s * 4 + h) * 8 : (s * 4 + h) * 8 + 8, :] = q[s * 8 : s * 8 + 8, h * 128 : h * 128 + 128]
    kn_s[0:32, :] = acc_kv[:, 0:128] + SCALE * d_qk[:, 512:640]
    vn_s[0:32, :] = acc_kv[:, 128:256] + SCALE * d_val

    for copy in cache:
        copy.wait()
    where = lax.broadcasted_iota(jnp.int32, (16, 1152), 1)
    step = lax.broadcasted_iota(jnp.int32, (16, 1152), 0) // 4
    fresh = jnp.logical_and(where >= 1024, where - 1024 <= step)
    factor = math.log2(math.e) / math.sqrt(HEAD_DIM)
    for b in range(8):
        k_v[b, 1024:1040, :] = kn_s[pl.ds(b, 16, stride=8), :].astype(BF16)
        v_v[b, 1024:1040, :] = vn_s[pl.ds(b, 16, stride=8), :].astype(BF16)
    for b in range(8):
        qb = q_s[pl.ds(b, 16, stride=8), :].astype(BF16)
        scores = lax.dot_general(qb, k_v[b], (((1,), (1,)), ((), ())), preferred_element_type=F32)
        seen = jnp.logical_or(where < lengths[b], fresh)
        scores = jnp.where(seen, scores, MASKED)
        top = jnp.max(scores, axis=-1, keepdims=True)
        weights = jnp.exp2((scores - top) * factor)
        total = jnp.sum(weights, axis=-1, keepdims=True)
        got = jnp.dot(weights.astype(BF16), v_v[b], preferred_element_type=F32)
        ctx_s[pl.ds(b, 16, stride=8), :] = got / total
    for s in range(4):
        for h in range(4):
            cx[s * 8 : s * 8 + 8, h * 128 : h * 128 + 128] = ctx_s[(s * 4 + h) * 8 : (s * 4 + h) * 8 + 8, :]
    context = cx[...].astype(BF16)

    for m in reversed(heads[:-1]):
        arrived(p2or.at[m], p2o_rs.at[m])
    for m in range(T):
        g, block = (m % 2) * 32, m // 2
        for j in range(2):
            tile = p2or[m, j * 48 : j * 48 + 32, :]
            at = j * 512 + block * 128
            uo_v[g : g + 32, at : at + 128] = tile
            uo_v[64 + g : 96 + g, at : at + 128] = tile
            do_v[m * 16 : m * 16 + 16, j * 128 : j * 128 + 128] = p2or[m, j * 48 + 32 : j * 48 + 48, :]
    halves = jnp.concatenate(
        [
            jnp.concatenate([context[:, 0:128], context[:, 128:256]], axis=0),
            jnp.concatenate([context[:, 256:384], context[:, 384:512]], axis=0),
        ],
        axis=1,
    )
    z_all = lax.dot_general(halves, do_v[...], (((1,), (1,)), ((), ())), preferred_element_type=F32)
    z = jnp.where(lane < 64, z_all[0:32], z_all[32:64])
    zs[...] = z.astype(BF16)
    for j, peer in enumerate(cross):
        send(zs, zr.at[t], z_ss.at[j], z_rs.at[t], peer)

    own = None
    for i in range(T):
        wo_copies[i].wait()
        part = jnp.dot(context, wo_v[i], preferred_element_type=F32)
        if i < T - 1:
            rss[i] = part.astype(BF16)
            send(rss.at[i], rsr.at[t], rs_ss.at[i], rs_rs.at[t], cross[i])
        else:
            own = part
    for m in reversed(heads[:-1]):
        arrived(zr.at[m], z_rs.at[m])
        z = z + zr[m].astype(F32)
    own = own + SCALE * jnp.dot(z.astype(BF16), uo_v[...], preferred_element_type=F32)
    for m in reversed(heads[:-1]):
        arrived(rsr.at[m], rs_rs.at[m])
        own = own + rsr[m].astype(F32)
    out_ref[...] = own.astype(BF16)
    for copy in sends:
        copy.wait_send()


def body(
    hidden, query_weight, keyval_weight, output_weight, adapter_down_stack, adapter_query_up,
    adapter_keyval_up, adapter_output_down, adapter_output_up, owner, key_cache_rows, value_cache_rows, lengths,
):
    steps, batch, width = hidden.shape
    rows = steps * batch
    anywhere = pl.BlockSpec(memory_space=pl.ANY)
    dma = pltpu.SemaphoreType.DMA
    out = pl.pallas_call(
        kernel,
        out_shape=pltpu.VMEM((rows, 1024), BF16),
        in_specs=[anywhere] * 13,
        out_specs=pl.BlockSpec(memory_space=pltpu.VMEM),
        scratch_shapes=[
            pltpu.VMEM((32, 8192), BF16),
            pltpu.VMEM((8192, 512), BF16),
            pltpu.VMEM((8192, 256), BF16),
            pltpu.VMEM((8, 512, 1024), BF16),
            pltpu.VMEM((8, 1152, 128), BF16),
            pltpu.VMEM((8, 1152, 128), BF16),
            pltpu.VMEM((3, 64, 128), BF16),
            pltpu.VMEM((2, 128, 128), BF16),
            pltpu.VMEM((64, 256), BF16),
            pltpu.VMEM((2, 64, 64), BF16),
            pltpu.VMEM((64, 256), BF16),
            pltpu.VMEM((64, 512), BF16),
            pltpu.VMEM((4, 64, 128), BF16),
            pltpu.VMEM((128, 128), BF16),
            pltpu.VMEM((16, 96, 128), BF16),
            pltpu.VMEM((16, 32, 128), BF16),
            pltpu.VMEM((16, 48, 128), BF16),
            pltpu.VMEM((32, 1024), BF16),
            pltpu.VMEM((1024, 256), BF16),
            pltpu.VMEM((8, 112, 128), BF16),
            pltpu.VMEM((8, 112, 128), BF16),
            pltpu.VMEM((8, 96, 128), BF16),
            pltpu.VMEM((8, 96, 128), BF16),
            pltpu.VMEM((128, 640), BF16),
            pltpu.VMEM((128, 128), BF16),
            pltpu.VMEM((128, 128), F32),
            pltpu.VMEM((128, 128), F32),
            pltpu.VMEM((128, 128), F32),
            pltpu.VMEM((32, 512), F32),
            pltpu.VMEM((32, 256), F32),
            pltpu.VMEM((128, 128), F32),
            pltpu.VMEM((32, 512), F32),
            pltpu.VMEM((128, 256), BF16),
            pltpu.VMEM((128, 1024), BF16),
            pltpu.VMEM((8, 32, 1024), BF16),
            pltpu.VMEM((8, 32, 1024), BF16),
            pltpu.VMEM((32, 128), BF16),
            pltpu.VMEM((8, 32, 128), BF16),
            pltpu.SMEM((R,), jnp.int32),
            pltpu.SMEM((8,), jnp.int32),
            dma((8,)), dma((K_PARTS,)), dma((2, K_PARTS)), dma((2,)), dma((T,)),
            dma((15,)), dma((R,)), dma((7,)), dma((R,)), dma((7,)), dma((R,)), dma((2,)), dma((2,)),
            dma((7,)), dma((T,)), dma((7,)), dma((T,)), dma((7,)), dma((T,)), dma((7,)), dma((T,)),
        ],
        compiler_params=pltpu.CompilerParams(
            collective_id=0, has_side_effects=True, vmem_limit_bytes=60 * 1024 * 1024
        ),
        name="adapter_attention",
    )(
        owner, lengths, hidden.reshape(rows, width), query_weight, keyval_weight, output_weight,
        jnp.swapaxes(adapter_down_stack, 1, 2), adapter_query_up, adapter_keyval_up, adapter_output_down.T,
        adapter_output_up, key_cache_rows, value_cache_rows,
    )
    return out.reshape(steps, batch, 1024)


def solution(mesh):
    in_specs = (
        P(None, "replica", None),
        P(None, "tensor"),
        P(None, None, "tensor"),
        P("tensor", None),
        P(None, "replica", None),
        P(None, "replica"),
        P(None, None, "replica"),
        P("replica", None),
        P(None, "replica"),
        P(),
        P("replica", None, "tensor"),
        P("replica", None, "tensor"),
        P("replica"),
    )
    out_specs = P(None, "replica", "tensor")
    return jax.shard_map(body, mesh=mesh, in_specs=in_specs, out_specs=out_specs, check_vma=False)
```

```python
import math

import jax
import jax.numpy as jnp
from jax import lax
from jax.experimental import pallas as pl
from jax.experimental.pallas import tpu as pltpu
from jax.sharding import PartitionSpec as P

MESH = pl.DeviceIdType.MESH
BF16 = jnp.bfloat16
F32 = jnp.float32
HEAD_DIM = 128
SCALE = 0.5
MASKED = -1e30
R, T = 16, 8
K_PARTS = 4


def kernel(
    owner_any, lengths_any, hid, wq, wkv, wo, dstk, qup, kvup, odn, oup, kc, vc,
    out_ref,
    hid_v, wq_v, wkv_v, wo_v, k_v, v_v, d_v, d_t, qup_v, kvup_v, odn_v, oup_v, upk, odp,
    p1d, p1u, p1o, hc, swap, dc, p2s, p2r, p2os, p2or,
    uqk, uv, q_s, acc_q, acc_kv, ctx_s, cx, do_v, uo_v, rss, rsr, zs, zr,
    owner, lengths, small_sem, q_sem, kv_sem, cache_sem, wo_sem,
    p1d_s, p1u_s, p1o_s, fwd_ss, fwd_rs, p2_s, p2o_s, rs_ss, rs_rs, z_s,
):
    r, t = lax.axis_index("replica"), lax.axis_index("tensor")
    x, zl, c = r // 4, lax.rem(r // 2, 2), lax.rem(r, 2)
    zh, y = t // 4, lax.rem(t, 4)
    other = (r + 1 - 2 * c, t)
    mine = c * 8 + r // 2
    chip = r // 2
    rows = 8192 // K_PARTS
    ring = [
        (lax.rem(x + dx, 4) * 4 + (zl if dz == 0 else 1 - zl) * 2 + c, t)
        for dx, dz in ((2, 1), (1, 1), (3, 1), (2, 0), (1, 0), (3, 0), (0, 1))
    ]
    heads = [
        (zh if dz == 0 else 1 - zh) * 4 + lax.rem(y + dy, 4)
        for dz, dy in ((1, 2), (1, 1), (1, 3), (0, 2), (1, 0), (0, 1), (0, 3), (0, 0))
    ]
    cross = [(r, to) for to in heads[:-1]]

    barrier = pltpu.get_barrier_semaphore()
    greeted = ring + [other] + cross
    for peer in greeted:
        pl.semaphore_signal(barrier, inc=1, device_id=peer, device_id_type=MESH)

    t128 = pl.multiple_of((t // 2) * 128, 128)
    small = [
        pltpu.make_async_copy(dstk.at[:, :, pl.ds(t128, 128)], d_v, small_sem.at[0]),
        pltpu.make_async_copy(qup, qup_v, small_sem.at[1]),
        pltpu.make_async_copy(kvup, kvup_v, small_sem.at[2]),
        pltpu.make_async_copy(odn, odn_v, small_sem.at[3]),
        pltpu.make_async_copy(oup, oup_v, small_sem.at[4]),
    ]
    hid_copy = pltpu.make_async_copy(hid, hid_v, small_sem.at[5])
    scalars = [
        pltpu.make_async_copy(owner_any, owner, small_sem.at[6]),
        pltpu.make_async_copy(lengths_any, lengths, small_sem.at[7]),
    ]
    for copy in small:
        copy.start()
    hid_copy.start()
    for copy in scalars:
        copy.start()

    def q_copies(i):
        at = pl.ds(pl.multiple_of(i * rows, rows), rows)
        return [
            pltpu.make_async_copy(wq.at[at, :], wq_v.at[at, :], q_sem.at[i]),
            pltpu.make_async_copy(wkv.at[0, at, :], wkv_v.at[at, pl.ds(0, 128)], kv_sem.at[0, i]),
            pltpu.make_async_copy(wkv.at[1, at, :], wkv_v.at[at, pl.ds(128, 128)], kv_sem.at[1, i]),
        ]

    for i in range(K_PARTS):
        for copy in q_copies(i):
            copy.start()

    k_v[:, 1056:1152, :] = jnp.zeros((4, 96, 256), BF16)
    v_v[:, 1056:1152, :] = jnp.zeros((4, 96, 256), BF16)
    uqk[0:64, 512:640] = jnp.zeros((64, 128), BF16)
    uqk[64:128, 0:512] = jnp.zeros((64, 512), BF16)

    for copy in small:
        copy.wait()
    lane = lax.broadcasted_iota(jnp.int32, (32, 128), 1)
    d_t[0] = jnp.concatenate([d_v[0], d_v[1]], axis=0).T
    d_t[1] = jnp.concatenate([d_v[2], d_v[2]], axis=0).T
    t64 = pl.multiple_of(lax.rem(t, 2) * 64, 64)
    p1d[chip, 0:64, :] = d_t[0, pl.ds(t64, 64), :]
    v_rows = d_t[1, pl.ds(t64, 64), :]
    p1d[chip, 64:96, :] = jnp.where(lane < 64, v_rows[0:32], v_rows[32:64])
    upk[0] = qup_v[:, 0:128]
    upk[1] = qup_v[:, 128:256]
    upk[2] = jnp.concatenate([kvup_v[0], kvup_v[1]], axis=1)
    upk[3] = jnp.zeros((64, 128), BF16)
    t32 = pl.multiple_of(lax.rem(t, 2) * 32, 32)
    p1u[mine] = upk[t // 2, pl.ds(t32, 32), :]
    odp[0:64, :] = odn_v[:, 0:128]
    odp[64:128, :] = odn_v[:, 128:256]
    p1o[mine, 0:32, :] = oup_v[pl.ds(t32, 32), pl.ds(t128, 128)]
    p1o[mine, 32:48, :] = odp[pl.ds(pl.multiple_of(t * 16, 16), 16), :]

    pl.semaphore_wait(barrier, len(greeted))

    sends = []

    def send(src, dst, ss, rs, peer, late=False):
        copy = pltpu.make_async_remote_copy(
            src_ref=src, dst_ref=dst, send_sem=ss, recv_sem=rs, device_id=peer, device_id_type=MESH
        )
        copy.start()
        if not late:
            sends.append(copy)

    def arrived(ref, sem):
        pltpu.make_async_copy(ref, ref, sem).wait()

    for j, peer in enumerate(ring):
        send(p1d.at[chip], p1d.at[chip], p1d_s.at[0], p1d_s.at[1], peer, late=True)
    for j, peer in enumerate(ring):
        send(p1u.at[mine], p1u.at[mine], p1u_s.at[0], p1u_s.at[1], peer, late=True)

    cache = [
        pltpu.make_async_copy(
            ref.at[b], to.at[b // 2, pl.ds(0, 1024), pl.ds(b % 2 * 128, 128)], cache_sem.at[j]
        )
        for j, ref, to in ((0, kc, k_v), (1, vc, v_v))
        for b in range(8)
    ]
    for copy in cache:
        copy.start()
    wo_copies = [
        pltpu.make_async_copy(
            wo.at[:, pl.ds(pl.multiple_of(heads[i] * 1024, 1024), 1024)], wo_v.at[i], wo_sem.at[i]
        )
        for i in range(T)
    ]
    for copy in wo_copies:
        copy.start()

    hid_copy.wait()
    odd = lax.rem(t, 2) == 1
    for g in range(8):
        first = hid_v[:, pl.ds(pl.multiple_of((2 * g) * 512 + t128, 128), 128)].astype(F32)
        second = hid_v[:, pl.ds(pl.multiple_of((2 * g + 1) * 512 + t128, 128), 128)].astype(F32)
        low = jnp.where(lane < 64, first, pltpu.roll(second, 64, 1))
        high = jnp.where(lane < 64, pltpu.roll(first, 64, 1), second)
        hc[0, :, g * 128 : (g + 1) * 128] = jnp.where(odd, high, low).astype(BF16)

    send(hc.at[0], hc.at[1], fwd_ss.at[2], fwd_rs.at[2], other)
    hc_copy = sends[-1]

    acc_q[...] = jnp.zeros_like(acc_q)
    acc_kv[...] = jnp.zeros_like(acc_kv)

    @pl.loop(0, K_PARTS)
    def _(i):
        for copy in q_copies(i):
            copy.wait()
        at = pl.ds(pl.multiple_of(i * rows, rows), rows)
        part = hid_v[:, at]
        acc_q[...] += jnp.dot(part, wq_v[at, :], preferred_element_type=F32)
        acc_kv[...] += jnp.dot(part, wkv_v[at, :], preferred_element_type=F32)

    for j, peer in enumerate(ring):
        send(p1o.at[mine], p1o.at[mine], p1o_s.at[0], p1o_s.at[1], peer, late=True)

    for copy in scalars:
        copy.wait()

    arrived(p1d.at[pl.ds(0, 7)], p1d_s.at[1])
    zero = jnp.zeros((32, 128), BF16)
    for s in range(R):
        held = lax.rem(owner[s], 2) == c
        tile = p1d[owner[s] // 2]
        top, bottom, dv = tile[0:32], tile[32:64], tile[64:96]
        dc[s * 64 : s * 64 + 32, 0:128] = jnp.where(held, top, zero)
        dc[s * 64 + 32 : s * 64 + 64, 0:128] = jnp.where(held, bottom, zero)
        dc[s * 64 : s * 64 + 32, 128:256] = jnp.where(jnp.logical_and(held, lane < 64), dv, zero)
        dc[s * 64 + 32 : s * 64 + 64, 128:256] = jnp.where(jnp.logical_and(held, lane >= 64), dv, zero)
    hc_copy.wait_recv()

    def packed(a):
        v = a[:, 128:256]
        v = v + pltpu.roll(v, 64, 1)
        return a[:, 0:128], jnp.where(lane[0:16] < 64, v[0:16], v[16:32])

    part_qk, part_v = packed(jnp.dot(hc[1], dc[...], preferred_element_type=F32))
    swap[0, 0:32, :] = part_qk.astype(BF16)
    swap[0, 32:48, :] = part_v.astype(BF16)
    send(swap.at[0], swap.at[1], fwd_ss.at[3], fwd_rs.at[3], other)
    swap_copy = sends[-1]
    part_qk, part_v = packed(jnp.dot(hc[0], dc[...], preferred_element_type=F32))

    same = pl.ds(pl.multiple_of(c * 8, 8), 8)
    arrived(p1u.at[pl.ds(0, 7)], p1u_s.at[1])
    send(p1u.at[same], p1u.at[same], fwd_ss.at[0], fwd_rs.at[0], other)
    u_copy = sends[-1]

    def slot_of(s):
        return lax.rem(owner[s], 2) * 8 + owner[s] // 2

    swap_copy.wait_recv()
    part_qk = (part_qk + swap[1, 0:32, :].astype(F32)).astype(BF16)
    part_v = (part_v + swap[1, 32:48, :].astype(F32)).astype(BF16)
    u_copy.wait_recv()
    for j, to in enumerate(heads):
        p2s[j, 0:32, :] = part_qk
        p2s[j, 32:48, :] = part_v
        p2s[j, 48:80, :] = p1u[slot_of(2 * to)]
        p2s[j, 80:112, :] = p1u[slot_of(2 * to + 1)]
        if j < 7:
            send(p2s.at[j], p2r.at[t], p2_s.at[0], p2_s.at[1], cross[j], late=True)
        else:
            p2r[t] = p2s[j]

    arrived(p1o.at[pl.ds(0, 7)], p1o_s.at[1])
    send(p1o.at[same], p1o.at[same], fwd_ss.at[1], fwd_rs.at[1], other)
    sends[-1].wait_recv()
    for j, to in enumerate(heads):
        p2os[j, 0:48, :] = p1o[slot_of(2 * to)]
        p2os[j, 48:96, :] = p1o[slot_of(2 * to + 1)]
        if j < 7:
            send(p2os.at[j], p2or.at[t], p2o_s.at[0], p2o_s.at[1], cross[j], late=True)
        else:
            p2or[t] = p2os[j]

    arrived(p2r.at[pl.ds(0, 7)], p2_s.at[1])
    a_qk = jnp.zeros((32, 128), F32)
    a_v = jnp.zeros((16, 128), F32)
    for m in range(T):
        a_qk = a_qk + p2r[m, 0:32, :].astype(F32)
        a_v = a_v + p2r[m, 32:48, :].astype(F32)
    for m in range(6):
        g, block = (m % 2) * 32, m // 2
        first, second = p2r[m, 48:80, :], p2r[m, 80:112, :]
        if block < 2:
            uqk[g : g + 32, block * 128 : block * 128 + 128] = first
            uqk[g : g + 32, 256 + block * 128 : 384 + block * 128] = second
        else:
            first, second = first.astype(F32), second.astype(F32)
            uk = jnp.where(lane < 64, first, pltpu.roll(second, 64, 1)).astype(BF16)
            uvt = jnp.where(lane < 64, pltpu.roll(first, 64, 1), second).astype(BF16)
            uqk[64 + g : 96 + g, 512:640] = uk
            uv[g : g + 32, :] = uvt
            uv[64 + g : 96 + g, :] = uvt
    low = lane[0:16] < 64
    a_v2 = jnp.concatenate([jnp.where(low, a_v, 0.0), jnp.where(low, 0.0, a_v)], axis=0)
    d_qk = jnp.dot(a_qk.astype(BF16), uqk[...], preferred_element_type=F32)
    d_val = jnp.dot(a_v2.astype(BF16), uv[...], preferred_element_type=F32)
    q = (acc_q[...] + SCALE * d_qk[:, 0:512]).astype(BF16).astype(F32)
    for s in range(4):
        for h in range(4):
            q_s[(s * 4 + h) * 8 : (s * 4 + h) * 8 + 8, :] = q[s * 8 : s * 8 + 8, h * 128 : h * 128 + 128]
    new_keys = (acc_kv[:, 0:128] + SCALE * d_qk[:, 512:640]).astype(BF16)
    new_values = (acc_kv[:, 128:256] + SCALE * d_val).astype(BF16)
    for pair in range(4):
        for j in range(2):
            k_v[pair, 1024:1056, j * 128 : j * 128 + 128] = new_keys
            v_v[pair, 1024:1056, j * 128 : j * 128 + 128] = new_values

    arrived(k_v.at[:, pl.ds(0, 1024), :], cache_sem.at[0])
    arrived(v_v.at[:, pl.ds(0, 1024), :], cache_sem.at[1])
    where = lax.broadcasted_iota(jnp.int32, (32, 1152), 1)
    row = lax.broadcasted_iota(jnp.int32, (32, 1152), 0)
    fresh = where - 1024
    known = jnp.logical_and(fresh >= 0, fresh // 8 <= lax.rem(row, 16) // 4)
    factor = math.log2(math.e) / math.sqrt(HEAD_DIM)
    blank = jnp.zeros((16, 128), BF16)
    for pair in range(4):
        b = 2 * pair
        q0 = q_s[pl.ds(b, 16, stride=8), :].astype(BF16)
        q1 = q_s[pl.ds(b + 1, 16, stride=8), :].astype(BF16)
        both = jnp.concatenate(
            [jnp.concatenate([q0, blank], axis=1), jnp.concatenate([blank, q1], axis=1)], axis=0
        )
        scores = lax.dot_general(both, k_v[pair], (((1,), (1,)), ((), ())), preferred_element_type=F32)
        live = jnp.where(row < 16, lengths[b], lengths[b + 1])
        seen = jnp.logical_or(
            where < live, jnp.logical_and(known, lax.rem(fresh, 8) == b + row // 16)
        )
        scores = jnp.where(seen, scores, MASKED)
        top = jnp.max(scores, axis=-1, keepdims=True)
        weights = jnp.exp2((scores - top) * factor)
        total = jnp.sum(weights, axis=-1, keepdims=True)
        got = jnp.dot(weights.astype(BF16), v_v[pair], preferred_element_type=F32) / total
        ctx_s[pl.ds(b, 16, stride=8), :] = got[0:16, 0:128]
        ctx_s[pl.ds(b + 1, 16, stride=8), :] = got[16:32, 128:256]
    for s in range(4):
        for h in range(4):
            cx[s * 8 : s * 8 + 8, h * 128 : h * 128 + 128] = ctx_s[(s * 4 + h) * 8 : (s * 4 + h) * 8 + 8, :]
    context = cx[...].astype(BF16)

    def adapter_sums():
        arrived(p2or.at[pl.ds(0, 7)], p2o_s.at[1])
        for m in range(T):
            g, block = (m % 2) * 32, m // 2
            for j in range(2):
                tile = p2or[m, j * 48 : j * 48 + 32, :]
                at = j * 512 + block * 128
                uo_v[g : g + 32, at : at + 128] = tile
                uo_v[64 + g : 96 + g, at : at + 128] = tile
                do_v[m * 16 : m * 16 + 16, j * 128 : j * 128 + 128] = p2or[m, j * 48 + 32 : j * 48 + 48, :]
        halves = jnp.concatenate(
            [
                jnp.concatenate([context[:, 0:128], context[:, 128:256]], axis=0),
                jnp.concatenate([context[:, 256:384], context[:, 384:512]], axis=0),
            ],
            axis=1,
        )
        z_all = lax.dot_general(halves, do_v[...], (((1,), (1,)), ((), ())), preferred_element_type=F32)
        z = jnp.where(lane < 64, z_all[0:32], z_all[32:64])
        zs[...] = z.astype(BF16)
        for j, peer in enumerate(cross):
            send(zs, zr.at[t], z_s.at[0], z_s.at[1], peer, late=True)
        return z

    own = None
    z = None
    for i in range(T):
        wo_copies[i].wait()
        part = jnp.dot(context, wo_v[i], preferred_element_type=F32)
        if i < T - 1:
            rss[i] = part.astype(BF16)
            send(rss.at[i], rsr.at[t], rs_ss.at[0], rs_rs.at[t], cross[i], late=True)
            if i == 3:
                z = adapter_sums()
        else:
            own = part
    for copy in sends:
        copy.wait_send()
    for ref, sem in ((p1d, p1d_s), (p1u, p1u_s), (p1o, p1o_s), (p2s, p2_s), (p2os, p2o_s), (zr, z_s)):
        arrived(ref.at[pl.ds(0, 7)], sem.at[0])
    arrived(zr.at[pl.ds(0, 7)], z_s.at[1])
    for m in heads[:-1]:
        z = z + zr[m].astype(F32)
    own = own + SCALE * jnp.dot(z.astype(BF16), uo_v[...], preferred_element_type=F32)
    for m in reversed(heads[:-1]):
        arrived(rsr.at[m], rs_rs.at[m])
        own = own + rsr[m].astype(F32)
    out_ref[...] = own.astype(BF16)
    arrived(rss.at[pl.ds(0, 7)], rs_ss.at[0])


def body(
    hidden, query_weight, keyval_weight, output_weight, adapter_down_stack, adapter_query_up,
    adapter_keyval_up, adapter_output_down, adapter_output_up, owner, key_cache_rows, value_cache_rows, lengths,
):
    steps, batch, width = hidden.shape
    rows = steps * batch
    anywhere = pl.BlockSpec(memory_space=pl.ANY)
    dma = pltpu.SemaphoreType.DMA
    out = pl.pallas_call(
        kernel,
        out_shape=pltpu.VMEM((rows, 1024), BF16),
        in_specs=[anywhere] * 13,
        out_specs=pl.BlockSpec(memory_space=pltpu.VMEM),
        scratch_shapes=[
            pltpu.VMEM((32, 8192), BF16),
            pltpu.VMEM((8192, 512), BF16),
            pltpu.VMEM((8192, 256), BF16),
            pltpu.VMEM((8, 512, 1024), BF16),
            pltpu.VMEM((4, 1152, 256), BF16),
            pltpu.VMEM((4, 1152, 256), BF16),
            pltpu.VMEM((3, 64, 128), BF16),
            pltpu.VMEM((2, 128, 128), BF16),
            pltpu.VMEM((64, 256), BF16),
            pltpu.VMEM((2, 64, 64), BF16),
            pltpu.VMEM((64, 256), BF16),
            pltpu.VMEM((64, 512), BF16),
            pltpu.VMEM((4, 64, 128), BF16),
            pltpu.VMEM((128, 128), BF16),
            pltpu.VMEM((8, 96, 128), BF16),
            pltpu.VMEM((16, 32, 128), BF16),
            pltpu.VMEM((16, 48, 128), BF16),
            pltpu.VMEM((2, 32, 1024), BF16),
            pltpu.VMEM((2, 48, 128), BF16),
            pltpu.VMEM((1024, 256), BF16),
            pltpu.VMEM((8, 112, 128), BF16),
            pltpu.VMEM((8, 112, 128), BF16),
            pltpu.VMEM((8, 96, 128), BF16),
            pltpu.VMEM((8, 96, 128), BF16),
            pltpu.VMEM((128, 640), BF16),
            pltpu.VMEM((128, 128), BF16),
            pltpu.VMEM((128, 128), F32),
            pltpu.VMEM((32, 512), F32),
            pltpu.VMEM((32, 256), F32),
            pltpu.VMEM((128, 128), F32),
            pltpu.VMEM((32, 512), F32),
            pltpu.VMEM((128, 256), BF16),
            pltpu.VMEM((128, 1024), BF16),
            pltpu.VMEM((8, 32, 1024), BF16),
            pltpu.VMEM((8, 32, 1024), BF16),
            pltpu.VMEM((32, 128), BF16),
            pltpu.VMEM((8, 32, 128), BF16),
            pltpu.SMEM((R,), jnp.int32),
            pltpu.SMEM((8,), jnp.int32),
            dma((8,)), dma((K_PARTS,)), dma((2, K_PARTS)), dma((2,)), dma((T,)),
            dma((2,)), dma((2,)), dma((2,)), dma((4,)), dma((4,)), dma((2,)), dma((2,)), dma((1,)), dma((T,)), dma((2,)),
        ],
        compiler_params=pltpu.CompilerParams(
            collective_id=0, has_side_effects=True, vmem_limit_bytes=60 * 1024 * 1024
        ),
        name="adapter_attention",
    )(
        owner, lengths, hidden.reshape(rows, width), query_weight, keyval_weight, output_weight,
        jnp.swapaxes(adapter_down_stack, 1, 2), adapter_query_up, adapter_keyval_up, adapter_output_down.T,
        adapter_output_up, key_cache_rows, value_cache_rows,
    )
    return out.reshape(steps, batch, 1024)


def solution(mesh):
    in_specs = (
        P(None, "replica", None),
        P(None, "tensor"),
        P(None, None, "tensor"),
        P("tensor", None),
        P(None, "replica", None),
        P(None, "replica"),
        P(None, None, "replica"),
        P("replica", None),
        P(None, "replica"),
        P(),
        P("replica", None, "tensor"),
        P("replica", None, "tensor"),
        P("replica"),
    )
    out_specs = P(None, "replica", "tensor")
    return jax.shard_map(body, mesh=mesh, in_specs=in_specs, out_specs=out_specs, check_vma=False)
```

```python
import math

import jax
import jax.numpy as jnp
from jax import lax
from jax.experimental import pallas as pl
from jax.experimental.pallas import tpu as pltpu
from jax.sharding import PartitionSpec as P

MESH = pl.DeviceIdType.MESH
BF16 = jnp.bfloat16
F32 = jnp.float32
HEAD_DIM = 128
SCALE = 0.5
MASKED = -1e30
R, T = 16, 8
K_PARTS = 4


def kernel(
    owner_any, lengths_any, hid, wq, wkv, wo, dstk, qup, kvup, odn, oup, kc, vc,
    out_ref,
    hid_v, wq_v, wkv_v, wo_v, k_v, v_v, d_v, d_t, qup_v, kvup_v, odn_v, oup_v, upk, odp,
    p1d, p1u, p1o, hc, swap, dc, p2s, p2r, p2os, p2or,
    uqk, uv, q_s, acc_q, acc_kv, ctx_s, cx, do_v, uo_v, rss, rsr, zs, zr,
    owner, lengths, small_sem, q_sem, kv_sem, cache_sem, wo_sem,
    p1d_s, p1u_s, p1o_s, fwd_ss, fwd_rs, p2_s, p2o_s, rs_ss, rs_rs, z_s,
):
    r, t = lax.axis_index("replica"), lax.axis_index("tensor")
    x, zl, c = r // 4, lax.rem(r // 2, 2), lax.rem(r, 2)
    zh, y = t // 4, lax.rem(t, 4)
    other = (r + 1 - 2 * c, t)
    mine = c * 8 + r // 2
    chip = r // 2
    rows = 8192 // K_PARTS
    ring = [
        (lax.rem(x + dx, 4) * 4 + (zl if dz == 0 else 1 - zl) * 2 + c, t)
        for dx, dz in ((2, 1), (1, 1), (3, 1), (2, 0), (1, 0), (3, 0), (0, 1))
    ]
    heads = []
    for first, second in zip([(1, 2), (1, 1), (1, 3), (0, 2), (1, 0), (0, 1), (0, 3), (0, 0)], [(0, 2), (1, 1), (1, 2), (1, 3), (0, 1), (1, 0), (0, 3), (0, 0)]):
        dz, dy = first[0] * (1 - c) + second[0] * c, first[1] * (1 - c) + second[1] * c
        heads.append(lax.rem(zh + dz, 2) * 4 + lax.rem(y + dy, 4))
    cross = [(r, to) for to in heads[:-1]]

    barrier = pltpu.get_barrier_semaphore()
    greeted = ring + [other] + cross
    for peer in greeted:
        pl.semaphore_signal(barrier, inc=1, device_id=peer, device_id_type=MESH)

    t128 = pl.multiple_of((t // 2) * 128, 128)
    small = [
        pltpu.make_async_copy(dstk.at[:, :, pl.ds(t128, 128)], d_v, small_sem.at[0]),
        pltpu.make_async_copy(qup, qup_v, small_sem.at[1]),
        pltpu.make_async_copy(kvup, kvup_v, small_sem.at[2]),
        pltpu.make_async_copy(odn, odn_v, small_sem.at[3]),
        pltpu.make_async_copy(oup, oup_v, small_sem.at[4]),
    ]
    hid_copy = pltpu.make_async_copy(hid, hid_v, small_sem.at[5])
    scalars = [
        pltpu.make_async_copy(owner_any, owner, small_sem.at[6]),
        pltpu.make_async_copy(lengths_any, lengths, small_sem.at[7]),
    ]
    for copy in small:
        copy.start()
    hid_copy.start()
    for copy in scalars:
        copy.start()

    def q_copies(i):
        at = pl.ds(pl.multiple_of(i * rows, rows), rows)
        return [
            pltpu.make_async_copy(wq.at[at, :], wq_v.at[at, :], q_sem.at[i]),
            pltpu.make_async_copy(wkv.at[0, at, :], wkv_v.at[at, pl.ds(0, 128)], kv_sem.at[0, i]),
            pltpu.make_async_copy(wkv.at[1, at, :], wkv_v.at[at, pl.ds(128, 128)], kv_sem.at[1, i]),
        ]

    for i in range(K_PARTS):
        for copy in q_copies(i):
            copy.start()

    k_v[:, 1056:1152, :] = jnp.zeros((4, 96, 256), BF16)
    v_v[:, 1056:1152, :] = jnp.zeros((4, 96, 256), BF16)
    uqk[0:64, 512:640] = jnp.zeros((64, 128), BF16)
    uqk[64:128, 0:512] = jnp.zeros((64, 512), BF16)

    for copy in small:
        copy.wait()
    lane = lax.broadcasted_iota(jnp.int32, (32, 128), 1)
    d_t[0] = jnp.concatenate([d_v[0], d_v[1]], axis=0).T
    d_t[1] = jnp.concatenate([d_v[2], d_v[2]], axis=0).T
    t64 = pl.multiple_of(lax.rem(t, 2) * 64, 64)
    p1d[chip, 0:64, :] = d_t[0, pl.ds(t64, 64), :]
    v_rows = d_t[1, pl.ds(t64, 64), :]
    p1d[chip, 64:96, :] = jnp.where(lane < 64, v_rows[0:32], v_rows[32:64])
    upk[0] = qup_v[:, 0:128]
    upk[1] = qup_v[:, 128:256]
    upk[2] = jnp.concatenate([kvup_v[0], kvup_v[1]], axis=1)
    upk[3] = jnp.zeros((64, 128), BF16)
    t32 = pl.multiple_of(lax.rem(t, 2) * 32, 32)
    p1u[mine] = upk[t // 2, pl.ds(t32, 32), :]
    odp[0:64, :] = odn_v[:, 0:128]
    odp[64:128, :] = odn_v[:, 128:256]
    p1o[mine, 0:32, :] = oup_v[pl.ds(t32, 32), pl.ds(t128, 128)]
    p1o[mine, 32:48, :] = odp[pl.ds(pl.multiple_of(t * 16, 16), 16), :]

    pl.semaphore_wait(barrier, len(greeted))

    sends = []

    def send(src, dst, ss, rs, peer, late=False):
        copy = pltpu.make_async_remote_copy(
            src_ref=src, dst_ref=dst, send_sem=ss, recv_sem=rs, device_id=peer, device_id_type=MESH
        )
        copy.start()
        if not late:
            sends.append(copy)

    def arrived(ref, sem):
        pltpu.make_async_copy(ref, ref, sem).wait()

    for j, peer in enumerate(ring):
        send(p1d.at[chip], p1d.at[chip], p1d_s.at[0], p1d_s.at[1], peer, late=True)
    for j, peer in enumerate(ring):
        send(p1u.at[mine], p1u.at[mine], p1u_s.at[0], p1u_s.at[1], peer, late=True)

    cache = [
        pltpu.make_async_copy(
            ref.at[b], to.at[b // 2, pl.ds(0, 1024), pl.ds(b % 2 * 128, 128)], cache_sem.at[j]
        )
        for j, ref, to in ((0, kc, k_v), (1, vc, v_v))
        for b in range(8)
    ]
    for copy in cache:
        copy.start()
    wo_copies = [
        pltpu.make_async_copy(
            wo.at[:, pl.ds(pl.multiple_of(heads[i] * 1024, 1024), 1024)], wo_v.at[i], wo_sem.at[0]
        )
        for i in range(T)
    ]
    for copy in wo_copies:
        copy.start()

    hid_copy.wait()
    odd = lax.rem(t, 2) == 1
    for g in range(8):
        first = hid_v[:, pl.ds(pl.multiple_of((2 * g) * 512 + t128, 128), 128)].astype(F32)
        second = hid_v[:, pl.ds(pl.multiple_of((2 * g + 1) * 512 + t128, 128), 128)].astype(F32)
        low = jnp.where(lane < 64, first, pltpu.roll(second, 64, 1))
        high = jnp.where(lane < 64, pltpu.roll(first, 64, 1), second)
        hc[0, :, g * 128 : (g + 1) * 128] = jnp.where(odd, high, low).astype(BF16)

    send(hc.at[0], hc.at[1], fwd_ss.at[2], fwd_rs.at[2], other)
    hc_copy = sends[-1]

    acc_q[...] = jnp.zeros_like(acc_q)
    acc_kv[...] = jnp.zeros_like(acc_kv)

    @pl.loop(0, K_PARTS)
    def _(i):
        for copy in q_copies(i):
            copy.wait()
        at = pl.ds(pl.multiple_of(i * rows, rows), rows)
        part = hid_v[:, at]
        acc_q[...] += jnp.dot(part, wq_v[at, :], preferred_element_type=F32)
        acc_kv[...] += jnp.dot(part, wkv_v[at, :], preferred_element_type=F32)

    for j, peer in enumerate(ring):
        send(p1o.at[mine], p1o.at[mine], p1o_s.at[0], p1o_s.at[1], peer, late=True)

    for copy in scalars:
        copy.wait()

    arrived(p1d.at[pl.ds(0, 7)], p1d_s.at[1])
    zero = jnp.zeros((32, 128), BF16)
    for s in range(R):
        held = lax.rem(owner[s], 2) == c
        tile = p1d[owner[s] // 2]
        top, bottom, dv = tile[0:32], tile[32:64], tile[64:96]
        dc[s * 64 : s * 64 + 32, 0:128] = jnp.where(held, top, zero)
        dc[s * 64 + 32 : s * 64 + 64, 0:128] = jnp.where(held, bottom, zero)
        dc[s * 64 : s * 64 + 32, 128:256] = jnp.where(jnp.logical_and(held, lane < 64), dv, zero)
        dc[s * 64 + 32 : s * 64 + 64, 128:256] = jnp.where(jnp.logical_and(held, lane >= 64), dv, zero)
    hc_copy.wait_recv()

    def packed(a):
        v = a[:, 128:256]
        v = v + pltpu.roll(v, 64, 1)
        return a[:, 0:128], jnp.where(lane[0:16] < 64, v[0:16], v[16:32])

    part_qk, part_v = packed(jnp.dot(hc[1], dc[...], preferred_element_type=F32))
    swap[0, 0:32, :] = part_qk.astype(BF16)
    swap[0, 32:48, :] = part_v.astype(BF16)
    send(swap.at[0], swap.at[1], fwd_ss.at[3], fwd_rs.at[3], other)
    swap_copy = sends[-1]
    part_qk, part_v = packed(jnp.dot(hc[0], dc[...], preferred_element_type=F32))

    same = pl.ds(pl.multiple_of(c * 8, 8), 8)
    arrived(p1u.at[pl.ds(0, 7)], p1u_s.at[1])
    send(p1u.at[same], p1u.at[same], fwd_ss.at[0], fwd_rs.at[0], other)
    u_copy = sends[-1]

    def slot_of(s):
        return lax.rem(owner[s], 2) * 8 + owner[s] // 2

    swap_copy.wait_recv()
    part_qk = (part_qk + swap[1, 0:32, :].astype(F32)).astype(BF16)
    part_v = (part_v + swap[1, 32:48, :].astype(F32)).astype(BF16)
    u_copy.wait_recv()
    for j, to in enumerate(heads):
        p2s[j, 0:32, :] = part_qk
        p2s[j, 32:48, :] = part_v
        p2s[j, 48:80, :] = p1u[slot_of(2 * to)]
        p2s[j, 80:112, :] = p1u[slot_of(2 * to + 1)]
        if j < 7:
            send(p2s.at[j], p2r.at[t], p2_s.at[0], p2_s.at[1], cross[j], late=True)
        else:
            p2r[t] = p2s[j]

    arrived(p1o.at[pl.ds(0, 7)], p1o_s.at[1])
    send(p1o.at[same], p1o.at[same], fwd_ss.at[1], fwd_rs.at[1], other)
    sends[-1].wait_recv()
    for j, to in enumerate(heads):
        p2os[j, 0:48, :] = p1o[slot_of(2 * to)]
        p2os[j, 48:96, :] = p1o[slot_of(2 * to + 1)]
        if j < 7:
            send(p2os.at[j], p2or.at[t], p2o_s.at[0], p2o_s.at[1], cross[j], late=True)
        else:
            p2or[t] = p2os[j]

    arrived(p2r.at[pl.ds(0, 7)], p2_s.at[1])
    a_qk = jnp.zeros((32, 128), F32)
    a_v = jnp.zeros((16, 128), F32)
    for m in range(T):
        a_qk = a_qk + p2r[m, 0:32, :].astype(F32)
        a_v = a_v + p2r[m, 32:48, :].astype(F32)
    for m in range(6):
        g, block = (m % 2) * 32, m // 2
        first, second = p2r[m, 48:80, :], p2r[m, 80:112, :]
        if block < 2:
            uqk[g : g + 32, block * 128 : block * 128 + 128] = first
            uqk[g : g + 32, 256 + block * 128 : 384 + block * 128] = second
        else:
            first, second = first.astype(F32), second.astype(F32)
            uk = jnp.where(lane < 64, first, pltpu.roll(second, 64, 1)).astype(BF16)
            uvt = jnp.where(lane < 64, pltpu.roll(first, 64, 1), second).astype(BF16)
            uqk[64 + g : 96 + g, 512:640] = uk
            uv[g : g + 32, :] = uvt
            uv[64 + g : 96 + g, :] = uvt
    low = lane[0:16] < 64
    a_v2 = jnp.concatenate([jnp.where(low, a_v, 0.0), jnp.where(low, 0.0, a_v)], axis=0)
    d_qk = jnp.dot(a_qk.astype(BF16), uqk[...], preferred_element_type=F32)
    d_val = jnp.dot(a_v2.astype(BF16), uv[...], preferred_element_type=F32)
    q = (acc_q[...] + SCALE * d_qk[:, 0:512]).astype(BF16).astype(F32)
    for s in range(4):
        for h in range(4):
            q_s[(s * 4 + h) * 8 : (s * 4 + h) * 8 + 8, :] = q[s * 8 : s * 8 + 8, h * 128 : h * 128 + 128]
    new_keys = (acc_kv[:, 0:128] + SCALE * d_qk[:, 512:640]).astype(BF16)
    new_values = (acc_kv[:, 128:256] + SCALE * d_val).astype(BF16)
    for pair in range(4):
        for j in range(2):
            k_v[pair, 1024:1056, j * 128 : j * 128 + 128] = new_keys
            v_v[pair, 1024:1056, j * 128 : j * 128 + 128] = new_values

    arrived(k_v.at[:, pl.ds(0, 1024), :], cache_sem.at[0])
    arrived(v_v.at[:, pl.ds(0, 1024), :], cache_sem.at[1])
    where = lax.broadcasted_iota(jnp.int32, (32, 1152), 1)
    row = lax.broadcasted_iota(jnp.int32, (32, 1152), 0)
    fresh = where - 1024
    known = jnp.logical_and(fresh >= 0, fresh // 8 <= lax.rem(row, 16) // 4)
    factor = math.log2(math.e) / math.sqrt(HEAD_DIM)
    blank = jnp.zeros((16, 128), BF16)
    for pair in range(4):
        b = 2 * pair
        q0 = q_s[pl.ds(b, 16, stride=8), :].astype(BF16)
        q1 = q_s[pl.ds(b + 1, 16, stride=8), :].astype(BF16)
        both = jnp.concatenate(
            [jnp.concatenate([q0, blank], axis=1), jnp.concatenate([blank, q1], axis=1)], axis=0
        )
        scores = lax.dot_general(both, k_v[pair], (((1,), (1,)), ((), ())), preferred_element_type=F32)
        live = jnp.where(row < 16, lengths[b], lengths[b + 1])
        seen = jnp.logical_or(
            where < live, jnp.logical_and(known, lax.rem(fresh, 8) == b + row // 16)
        )
        scores = jnp.where(seen, scores, MASKED)
        top = jnp.max(scores, axis=-1, keepdims=True)
        weights = jnp.exp2((scores - top) * factor)
        total = jnp.sum(weights, axis=-1, keepdims=True)
        got = jnp.dot(weights.astype(BF16), v_v[pair], preferred_element_type=F32) / total
        ctx_s[pl.ds(b, 16, stride=8), :] = got[0:16, 0:128]
        ctx_s[pl.ds(b + 1, 16, stride=8), :] = got[16:32, 128:256]
    for s in range(4):
        for h in range(4):
            cx[s * 8 : s * 8 + 8, h * 128 : h * 128 + 128] = ctx_s[(s * 4 + h) * 8 : (s * 4 + h) * 8 + 8, :]
    context = cx[...].astype(BF16)

    def adapter_sums():
        arrived(p2or.at[pl.ds(0, 7)], p2o_s.at[1])
        for m in range(T):
            g, block = (m % 2) * 32, m // 2
            for j in range(2):
                tile = p2or[m, j * 48 : j * 48 + 32, :]
                at = j * 512 + block * 128
                uo_v[g : g + 32, at : at + 128] = tile
                uo_v[64 + g : 96 + g, at : at + 128] = tile
                do_v[m * 16 : m * 16 + 16, j * 128 : j * 128 + 128] = p2or[m, j * 48 + 32 : j * 48 + 48, :]
        halves = jnp.concatenate(
            [
                jnp.concatenate([context[:, 0:128], context[:, 128:256]], axis=0),
                jnp.concatenate([context[:, 256:384], context[:, 384:512]], axis=0),
            ],
            axis=1,
        )
        z_all = lax.dot_general(halves, do_v[...], (((1,), (1,)), ((), ())), preferred_element_type=F32)
        z = jnp.where(lane < 64, z_all[0:32], z_all[32:64])
        zs[...] = z.astype(BF16)
        for j, peer in enumerate(cross):
            send(zs, zr.at[t], z_s.at[0], z_s.at[1], peer, late=True)
        return z

    arrived(wo_v, wo_sem.at[0])

    own = None
    z = None
    for i in range(T):
        part = jnp.dot(context, wo_v[i], preferred_element_type=F32)
        if i < T - 1:
            rss[i] = part.astype(BF16)
            send(rss.at[i], rsr.at[t], rs_ss.at[0], rs_rs.at[t], cross[i], late=True)
            if i == 3:
                z = adapter_sums()
        else:
            own = part
    for copy in sends:
        copy.wait_send()
    for ref, sem in ((p1d, p1d_s), (p1u, p1u_s), (p1o, p1o_s), (p2s, p2_s), (p2os, p2o_s), (zr, z_s)):
        arrived(ref.at[pl.ds(0, 7)], sem.at[0])
    arrived(zr.at[pl.ds(0, 7)], z_s.at[1])
    for m in heads[:-1]:
        z = z + zr[m].astype(F32)
    own = own + SCALE * jnp.dot(z.astype(BF16), uo_v[...], preferred_element_type=F32)
    for m in reversed(heads[:-1]):
        arrived(rsr.at[m], rs_rs.at[m])
        own = own + rsr[m].astype(F32)
    out_ref[...] = own.astype(BF16)
    arrived(rss.at[pl.ds(0, 7)], rs_ss.at[0])


def body(
    hidden, query_weight, keyval_weight, output_weight, adapter_down_stack, adapter_query_up,
    adapter_keyval_up, adapter_output_down, adapter_output_up, owner, key_cache_rows, value_cache_rows, lengths,
):
    steps, batch, width = hidden.shape
    rows = steps * batch
    anywhere = pl.BlockSpec(memory_space=pl.ANY)
    dma = pltpu.SemaphoreType.DMA
    out = pl.pallas_call(
        kernel,
        out_shape=pltpu.VMEM((rows, 1024), BF16),
        in_specs=[anywhere] * 13,
        out_specs=pl.BlockSpec(memory_space=pltpu.VMEM),
        scratch_shapes=[
            pltpu.VMEM((32, 8192), BF16),
            pltpu.VMEM((8192, 512), BF16),
            pltpu.VMEM((8192, 256), BF16),
            pltpu.VMEM((8, 512, 1024), BF16),
            pltpu.VMEM((4, 1152, 256), BF16),
            pltpu.VMEM((4, 1152, 256), BF16),
            pltpu.VMEM((3, 64, 128), BF16),
            pltpu.VMEM((2, 128, 128), BF16),
            pltpu.VMEM((64, 256), BF16),
            pltpu.VMEM((2, 64, 64), BF16),
            pltpu.VMEM((64, 256), BF16),
            pltpu.VMEM((64, 512), BF16),
            pltpu.VMEM((4, 64, 128), BF16),
            pltpu.VMEM((128, 128), BF16),
            pltpu.VMEM((8, 96, 128), BF16),
            pltpu.VMEM((16, 32, 128), BF16),
            pltpu.VMEM((16, 48, 128), BF16),
            pltpu.VMEM((2, 32, 1024), BF16),
            pltpu.VMEM((2, 48, 128), BF16),
            pltpu.VMEM((1024, 256), BF16),
            pltpu.VMEM((8, 112, 128), BF16),
            pltpu.VMEM((8, 112, 128), BF16),
            pltpu.VMEM((8, 96, 128), BF16),
            pltpu.VMEM((8, 96, 128), BF16),
            pltpu.VMEM((128, 640), BF16),
            pltpu.VMEM((128, 128), BF16),
            pltpu.VMEM((128, 128), F32),
            pltpu.VMEM((32, 512), F32),
            pltpu.VMEM((32, 256), F32),
            pltpu.VMEM((128, 128), F32),
            pltpu.VMEM((32, 512), F32),
            pltpu.VMEM((128, 256), BF16),
            pltpu.VMEM((128, 1024), BF16),
            pltpu.VMEM((8, 32, 1024), BF16),
            pltpu.VMEM((8, 32, 1024), BF16),
            pltpu.VMEM((32, 128), BF16),
            pltpu.VMEM((8, 32, 128), BF16),
            pltpu.SMEM((R,), jnp.int32),
            pltpu.SMEM((8,), jnp.int32),
            dma((8,)), dma((K_PARTS,)), dma((2, K_PARTS)), dma((2,)), dma((1,)),
            dma((2,)), dma((2,)), dma((2,)), dma((4,)), dma((4,)), dma((2,)), dma((2,)), dma((1,)), dma((T,)), dma((2,)),
        ],
        compiler_params=pltpu.CompilerParams(
            collective_id=0, has_side_effects=True, vmem_limit_bytes=60 * 1024 * 1024
        ),
        name="adapter_attention",
    )(
        owner, lengths, hidden.reshape(rows, width), query_weight, keyval_weight, output_weight,
        jnp.swapaxes(adapter_down_stack, 1, 2), adapter_query_up, adapter_keyval_up, adapter_output_down.T,
        adapter_output_up, key_cache_rows, value_cache_rows,
    )
    return out.reshape(steps, batch, 1024)


def solution(mesh):
    in_specs = (
        P(None, "replica", None),
        P(None, "tensor"),
        P(None, None, "tensor"),
        P("tensor", None),
        P(None, "replica", None),
        P(None, "replica"),
        P(None, None, "replica"),
        P("replica", None),
        P(None, "replica"),
        P(),
        P("replica", None, "tensor"),
        P("replica", None, "tensor"),
        P("replica"),
    )
    out_specs = P(None, "replica", "tensor")
    return jax.shard_map(body, mesh=mesh, in_specs=in_specs, out_specs=out_specs, check_vma=False)
```
